32 devices in a mesh: lon: 8 (over y, x, core), lat: 4 (over z).
Axes of the slice: x: 2, y: 2, z: 4, core: 2. Of those that a mesh axis runs over, the one named last changes fastest.
Arguments:
- state: float32 [75, 4, 64, 1024], P(None, None, 'lat', 'lon'), may hold values from -6 to 6
- depth_levels: int32 [64, 1024], P('lat', 'lon'), may hold values from 0 to 75, as said below
Outputs:
- new_state: float32 [75, 4, 64, 1024], P(None, None, 'lat', 'lon')
The draws below stay inside these ranges and needn't reach their ends.
Inputs may be any that keep to these rules, and one draw needn't show every extreme that they name: `depth_levels`: the number of wet levels of each column; land (0) grows more common eastward.
All inputs are finite; a program needn't handle non-finite values.
Results may differ from the reference program's by a relative error of at most 0.000059.
Values sent between devices are 32-bit elements; how exact they have to be, the bound alone decides.
No kernel may reach another device: no remote copies, remote signals or barrier semaphores. Data moves between devices by JAX's collectives and lax.ppermute only.
A program may use at most 192 MiB of HBM per device.

```python
import jax
import jax.numpy as jnp
from jax import lax

NZ = 75
STEPS = 2
NX = 1024
NY = 64


def draw_depth_levels(key, part):
    level_key = jax.random.fold_in(key, 11)
    land_key = jax.random.fold_in(key, 23)
    levels = jax.random.randint(level_key, (NY, NX), 1, NZ + 1)
    columns = jnp.arange(NX, dtype=jnp.int32)[None, :]
    levels = jnp.where(columns == 0, NZ, levels)
    chance = jax.random.randint(land_key, (NY, NX), 0, 100)
    land = chance < 70 * columns // NX
    rows = jnp.arange(NY, dtype=jnp.int32)[:, None]
    land = jnp.logical_or(land, jnp.logical_and(rows == 0, columns == NX - 1))
    return jnp.where(land, 0, levels).astype(jnp.int32)


def block_scale(key, shape, shards, smallest, largest):
    level = 1.0
    for axis_at, blocks in shards:
        steps = jax.random.uniform(jax.random.fold_in(jax.random.fold_in(key, 6), axis_at), (blocks,), jnp.float32, smallest / len(shards), largest / len(shards))
        level = level * jnp.repeat(jnp.exp(steps), shape[axis_at] // blocks).reshape((-1,) + (1,) * (len(shape) - 1 - axis_at))
    return level


def centred(key, extent, deviation, bound, cuts=(), held_as=jnp.bfloat16):
    values = jax.random.normal(key, extent, jnp.float32) * deviation
    if len(cuts) > 0:
        values = block_scale(key, extent, cuts, -0.22, 0.18) * values
    return jnp.clip(values, min=-bound, max=bound).astype(held_as)


def setup_inputs(seed: int = 0) -> dict:
    seeds = jax.random.split(jax.random.key(seed), 3)
    state = centred(seeds[0], (NZ, 4, NY, NX), 1.0, 6.0, ((2, 4), (3, 8)), jnp.float32)
    depth_levels = draw_depth_levels(jax.random.fold_in(seeds[2], 71), 0)
    return dict(state=state, depth_levels=depth_levels)


ADVECTION = 0.25
SPREADING = 0.15
VERTICAL_MIX = 64.0


def wet_levels(depth_levels, levels):
    level_index = lax.broadcasted_iota(jnp.int32, (levels,) + depth_levels.shape, 0)
    return (level_index < depth_levels[None]).astype(jnp.float32)


def coriolis_rows(first_row, row_count, total_rows):
    row_index = first_row + jnp.arange(row_count, dtype=jnp.int32)
    mirrored = jnp.where(row_index >= total_rows, 2 * total_rows - 1 - row_index, row_index)
    return 0.1 + 0.4 * (mirrored.astype(jnp.float32) + 0.5) / total_rows


def sign_table(dtype):
    return jnp.array([1.0, 1.0, -1.0, -1.0, 1.0], dtype)


def tridiagonal_columns(provisional, wet_centre):
    zero_level = jnp.zeros_like(wet_centre[:1])
    below = jnp.concatenate([wet_centre[1:], zero_level], axis=0)
    above = jnp.concatenate([zero_level, wet_centre[:-1]], axis=0)
    lower_coef = VERTICAL_MIX * wet_centre * above
    upper_coef = VERTICAL_MIX * wet_centre * below
    diagonal = 1.0 + lower_coef + upper_coef

    def forward(carried, level_terms):
        prev_upper, prev_value = carried
        lower_k, diag_k, upper_k, value_k = level_terms
        denominator = diag_k - lower_k * prev_upper
        next_upper = upper_k / denominator
        next_value = (value_k - lower_k * prev_value) / denominator
        return (next_upper, next_value), (next_upper, next_value)

    start = (jnp.zeros_like(wet_centre[0]), jnp.zeros_like(provisional[0]))
    _, (upper_all, value_all) = lax.scan(forward, start, (lower_coef, diagonal, upper_coef, provisional))

    def backward(next_solution, level_terms):
        upper_k, value_k = level_terms
        solution = value_k - upper_k * next_solution
        return solution, solution

    _, solved = lax.scan(backward, jnp.zeros_like(provisional[0]), (upper_all, value_all), reverse=True)
    return solved


def advance(padded, coriolis):
    height = padded.shape[2] - 2
    breadth = padded.shape[3] - 2

    def shifted(array, row_off, col_off):
        return array[:, :, 1 + row_off:1 + row_off + height, 1 + col_off:1 + col_off + breadth]

    centre = shifted(padded, 0, 0)
    east_cell = shifted(padded, 0, 1)
    west_cell = shifted(padded, 0, -1)
    north_cell = shifted(padded, 1, 0)
    south_cell = shifted(padded, -1, 0)
    density = (-0.25 * padded[:, 0] + 0.75 * padded[:, 1]) * padded[:, 4]
    pressure = (0.2 * jnp.cumsum(density, axis=0))[:, None]
    grad_east = shifted(pressure, 0, 1)[:, 0] - shifted(pressure, 0, -1)[:, 0]
    grad_north = shifted(pressure, 1, 0)[:, 0] - shifted(pressure, -1, 0)[:, 0]
    values = centre[:, 0:4]
    wet_centre = centre[:, 4:5]
    flux_sum = (east_cell[:, 2:3] * east_cell[:, 0:4] - west_cell[:, 2:3] * west_cell[:, 0:4]
                + north_cell[:, 3:4] * north_cell[:, 0:4] - south_cell[:, 3:4] * south_cell[:, 0:4])
    spread = (east_cell[:, 4:5] * (east_cell[:, 0:4] - values) + west_cell[:, 4:5] * (west_cell[:, 0:4] - values)
              + north_cell[:, 4:5] * (north_cell[:, 0:4] - values) + south_cell[:, 4:5] * (south_cell[:, 0:4] - values))
    rotation = coriolis[1:1 + height][None, :, None]
    force_east = rotation * values[:, 3] - 0.5 * grad_east
    force_north = -rotation * values[:, 2] - 0.5 * grad_north
    forcing = jnp.concatenate([jnp.zeros_like(values[:, 0:2]), force_east[:, None], force_north[:, None]], axis=1)
    provisional = wet_centre * (values - ADVECTION * flux_sum + SPREADING * spread + forcing)
    return tridiagonal_columns(provisional, wet_centre)


def extend_global(full, halo_width):
    with_lon = jnp.concatenate([full[..., -halo_width:], full, full[..., :halo_width]], axis=3)
    total_rows = full.shape[2]
    folded = with_lon[:, :, total_rows - halo_width:, :][:, :, ::-1, ::-1] * sign_table(full.dtype)[None, :, None, None]
    southern = jnp.zeros_like(with_lon[:, :, :halo_width, :])
    return jnp.concatenate([southern, with_lon, folded], axis=2)


def reference(state, depth_levels):
    wet_field = wet_levels(depth_levels, state.shape[0]).astype(state.dtype)
    total_rows = state.shape[2]
    coriolis = coriolis_rows(-1, total_rows + 2, total_rows).astype(state.dtype)
    current = state
    for step_index in range(STEPS):
        full = jnp.concatenate([current, wet_field[:, None]], axis=1)
        current = advance(extend_global(full, 1), coriolis)
    return current
```

```python
import functools

import jax
import jax.numpy as jnp
import numpy as np
from jax import lax
from jax.experimental import pallas as pl
from jax.experimental.pallas import tpu as pltpu
from jax.sharding import PartitionSpec as P

STEPS = 2
VERTICAL_MIX = 64.0
GROUP = 8
SUB = 8
PAD = 8
CHUNKS = 10
VMEM_LIMIT = 40 * 1024 * 1024


def elimination_table(levels):
    inside = np.zeros(levels)
    last = np.zeros(levels)
    upper = 0.0
    for k in range(levels):
        lower = VERTICAL_MIX if k else 0.0
        inside[k] = 1.0 / (1.0 + lower + VERTICAL_MIX - lower * upper)
        last[k] = 1.0 / (1.0 + lower - lower * upper)
        upper = VERTICAL_MIX * inside[k]
    return (np.stack([inside, last]) / 4).astype(np.float32)


def tile_pair(value, c, half):
    return value[c][half * SUB : (half + 1) * SUB, :]


def pack_columns(acc, values, slot, lane):
    for c in range(len(values)):
        for half in range(2):
            place = GROUP * slot + 2 * c + half
            turned = pltpu.roll(tile_pair(values, c, half), 2 * place + 1, axis=1)
            acc = jnp.where((lane >> 1) == place, turned, acc)
    return acc


def write_rows(state_ref, depth, outer_ref, inner_ref, channels, height, tiles=None):
    at_lat = lax.axis_index("lat")
    even = lax.rem(at_lat, 2) == 0
    fold = at_lat == lax.axis_size("lat") - 1
    shape = (SUB, 128)
    reverse = 127 - lax.broadcasted_iota(jnp.int32, shape, 1)
    line = lax.broadcasted_iota(jnp.int32, shape, 0)
    sign = jnp.where(lax.rem(line, channels) >= 2, -1.0, 1.0)
    rows = (state_ref.shape[0] - 2 * PAD) // height
    for start in tiles or range(0, rows, SUB):
        count = min(SUB, rows - start)
        at = pl.ds(start, SUB)
        base = PAD + start * height
        top = state_ref[pl.ds(base + height - 1, count, stride=height), :]
        bottom = state_ref[pl.ds(base, count, stride=height), :]
        if count < SUB:
            top = jnp.concatenate([top, jnp.broadcast_to(depth[-1:], (SUB - count, 128))], axis=0)
            bottom = jnp.concatenate([bottom, jnp.broadcast_to(depth[:1], (SUB - count, 128))], axis=0)
            sign = jnp.where(line >= count, 1.0, sign)
        mirrored = jnp.take_along_axis(top, reverse, axis=1) * sign
        outer_ref[at, :] = jnp.where(even, top, bottom)
        inner_ref[at, :] = jnp.where(even, bottom, jnp.where(fold, mirrored, top))


def zero_pads(ref):
    pad = jnp.zeros((PAD, 128), jnp.float32)
    ref[pl.ds(0, PAD), :] = pad
    ref[pl.ds(ref.shape[0] - PAD, PAD), :] = pad


def pack_kernel(levels, channels, height, state_hbm, levels_hbm, state_ref, depth_ref, columns_ref, outer_ref, inner_ref, levels_ref, sems):
    lane = lax.broadcasted_iota(jnp.int32, (SUB, 128), 1)
    level_rows = channels * height
    whole, rest = divmod(levels, GROUP)
    groups = whole + 1
    per_chunk = pl.cdiv(groups, CHUNKS)
    copies = []
    for n, first_group in enumerate(range(0, groups, per_chunk)):
        first_level = first_group * GROUP
        count = min(per_chunk * GROUP, levels - first_level) * level_rows
        copies.append(
            pltpu.make_async_copy(
                state_hbm.at[pl.ds(first_level * level_rows, count), :],
                state_ref.at[pl.ds(PAD + first_level * level_rows, count), :],
                sems.at[n],
            )
        )
    depth_copy = pltpu.make_async_copy(levels_hbm, levels_ref, sems.at[CHUNKS])
    depth_copy.start()
    for copy in copies:
        copy.start()
    zero_pads(state_ref)
    depth_copy.wait()
    depth = levels_ref[...].astype(jnp.float32)
    depth_ref[...] = depth
    empty = jnp.zeros((SUB, 128), jnp.float32)

    def group(g, count, acc):
        for slot in range(count):
            base = PAD + (g * GROUP + slot) * level_rows
            values = [state_ref[pl.ds(base + c * height, height), :] for c in range(channels)]
            acc = pack_columns(acc, values, slot, lane)
        columns_ref[g] = acc

    rows = levels * channels
    step = per_chunk * GROUP * channels
    for n, copy in enumerate(copies):
        copy.wait()
        for g in range(n * per_chunk, min((n + 1) * per_chunk, groups)):
            if g < whole:
                group(g, GROUP, empty)
            else:
                group(g, rest, pack_columns(empty, [depth], rest, lane))
        tiles = range(n * step, min((n + 1) * step, rows), SUB)
        write_rows(state_ref, depth, outer_ref, inner_ref, channels, height, tiles)


def interior_kernel(levels, channels, height, table_ref, state_ref, depth_ref, sum_ref, inverse_ref, pressure_ref):
    whole, rest = divmod(levels, GROUP)
    level_rows = channels * height
    full = (height, 128)
    column = lax.broadcasted_iota(jnp.int32, full, 1)
    row = lax.broadcasted_iota(jnp.int32, full, 0)
    at_west, at_east = column == 0, column == 127
    at_south, at_north = row == 0, row == height - 1
    at_lat = lax.axis_index("lat")
    total = height * lax.axis_size("lat")
    rotation = 0.4 + 1.6 * ((at_lat * height + row).astype(jnp.float32) + 0.5) / total
    depth = depth_ref[...]
    depth_east = jnp.where(at_east, 0.0, pltpu.roll(depth, 127, axis=1))
    depth_west = jnp.where(at_west, 0.0, pltpu.roll(depth, 1, axis=1))
    depth_north = jnp.where(at_north, 0.0, pltpu.roll(depth, height - 1, axis=0))
    depth_south = jnp.where(at_south, 0.0, pltpu.roll(depth, 1, axis=0))
    last_level = depth - 1.0
    slot_rows = height + 2 * PAD
    pad = jnp.zeros((PAD, 128), jnp.float32)
    for slot in range(GROUP):
        pressure_ref[pl.ds(slot * slot_rows, PAD), :] = pad
        pressure_ref[pl.ds(slot * slot_rows + PAD + height, PAD), :] = pad

    def group(g, count, pressure):
        for slot in range(count):
            k = g * GROUP + slot
            level = jnp.asarray(k, jnp.float32)
            inverse_ref[pl.ds(k * height, height), :] = jnp.where(
                last_level > level,
                table_ref[0, k],
                jnp.where(last_level == level, table_ref[1, k], 0.0),
            )
            base = PAD + (g * GROUP + slot) * level_rows

            def rows_at(c, shift):
                return state_ref[pl.ds(base + c * height + shift, height), :]

            values = [rows_at(c, 0) for c in range(channels)]
            pressure = pressure + jnp.where(depth > level, 0.3 * values[1] - 0.1 * values[0], 0.0)
            at = slot * slot_rows + PAD
            pressure_ref[pl.ds(at, height), :] = pressure
            slope_east = jnp.where(at_east, 0.0, pltpu.roll(pressure, 127, axis=1)) - jnp.where(
                at_west, 0.0, pltpu.roll(pressure, 1, axis=1)
            )
            slope_north = pressure_ref[pl.ds(at + 1, height), :] - pressure_ref[pl.ds(at - 1, height), :]
            east = [pltpu.roll(v, 127, axis=1) for v in values]
            west = [pltpu.roll(v, 1, axis=1) for v in values]
            north = [rows_at(c, 1) for c in range(channels)]
            south = [rows_at(c, -1) for c in range(channels)]
            weights = [
                jnp.where(d > level, 0.6, 0.0) for d in (depth_east, depth_west, depth_north, depth_south)
            ]
            from_east = jnp.where(at_east, 0.0, weights[0] - east[2])
            from_west = jnp.where(at_west, 0.0, weights[1] + west[2])
            from_north = jnp.where(at_north, 0.0, weights[2] - north[3])
            from_south = jnp.where(at_south, 0.0, weights[3] + south[3])
            centre = 4.0 - ((weights[0] + weights[1]) + (weights[2] + weights[3]))
            forces = [None, None, rotation * values[3] - slope_east, -rotation * values[2] - slope_north]
            for c in range(channels):
                moved = (centre * values[c] + from_east * east[c]) + (
                    from_west * west[c] + from_north * north[c]
                )
                moved = moved + from_south * south[c]
                if forces[c] is not None:
                    moved = moved + forces[c]
                sum_ref[pl.ds((g * GROUP + slot) * level_rows + c * height, height), :] = moved
        return pressure

    pressure = jnp.zeros(full, jnp.float32)
    for g in range(whole + 1):
        pressure = group(g, GROUP if g < whole else rest, pressure)


def halo_rows(levels, channels, height, state_ref, one_ref, two_ref, northern, out_ref):
    edge = height - 1 if northern else 0
    way = -1.0 if northern else 1.0

    at_lat = lax.axis_index("lat")
    even = lax.rem(at_lat, 2) == 0

    def halo(at, count, stride):
        one = one_ref[pl.ds(at, count, stride=stride), :]
        two = two_ref[pl.ds(at, count, stride=stride), :]
        if northern:
            return jnp.where(even, one, two)
        return jnp.where(even, jnp.where(at_lat == 0, 0.0, two), one)

    depth = halo(channels * levels, 1, 1)
    carry = jnp.zeros((1, 128), jnp.float32)
    for start in range(0, levels, SUB):
        count = min(SUB, levels - start)
        near = [halo(channels * start + c, count, channels) for c in range(channels)]
        level = lax.broadcasted_iota(jnp.int32, (count, 128), 0)
        wet = (level + start).astype(jnp.float32) < depth
        weight = jnp.where(wet, 0.6, 0.0)
        pressure = jnp.where(wet, 0.3 * near[1] - 0.1 * near[0], 0.0)
        if count < SUB:
            pressure = jnp.concatenate([pressure, jnp.zeros((SUB - count, 128), jnp.float32)], axis=0)
        level = lax.broadcasted_iota(jnp.int32, (SUB, 128), 0)
        for shift in (1, 2, 4):
            pressure = pressure + jnp.where(level >= shift, pltpu.roll(pressure, shift, axis=0), 0.0)
        pressure = pressure + carry
        carry = pressure[SUB - 1 : SUB, :]
        factor = weight + way * near[3]
        for c in range(channels):
            at = PAD + (start * channels + c) * height + edge
            own = state_ref[pl.ds(at, count, stride=channels * height), :]
            added = factor * near[c] - weight * own
            if c == 3:
                added = added + way * pressure[:count]
            out_ref[pl.ds(start * channels + c, count, stride=channels), :] = added


def halo_columns(levels, channels, own_ref, one_ref, two_ref, out_ref):
    assert channels == 4 and GROUP == 8
    shape = (SUB, 128)
    lane = lax.broadcasted_iota(jnp.int32, shape, 1)
    western = (lane & 1) == 1
    way = jnp.where(western, 1.0, -1.0)
    channel = (lane >> 2) & 3
    slot = lane >> 4

    even = lax.rem(lax.axis_index("lon"), 2) == 0

    def halo(g):
        one, two = one_ref[g], two_ref[g]
        east = jnp.where(even, one, two)
        west = jnp.where(even, two, one)
        return jnp.where(western, pltpu.roll(west, 1, axis=1), pltpu.roll(east, 127, axis=1))

    whole, rest = divmod(levels, GROUP)
    groups = whole + 1
    near = [halo(g) for g in range(groups)]
    depth = jnp.where(lane >> 2 == channels * rest, near[whole], 0.0)
    for shift in (4, 8, 16, 32, 64):
        depth = depth + pltpu.roll(depth, shift, axis=1)
    carry = jnp.zeros(shape, jnp.float32)
    for g in range(groups):
        wet = (slot + g * GROUP).astype(jnp.float32) < depth
        weight = jnp.where(wet, 0.6, 0.0)
        velocity = jnp.where(channel == 2, near[g], 0.0)
        velocity = velocity + pltpu.roll(velocity, 4, axis=1)
        velocity = velocity + pltpu.roll(velocity, 120, axis=1)
        pressure = 0.3 * pltpu.roll(near[g], 124, axis=1) - 0.1 * near[g]
        pressure = jnp.where(jnp.logical_and(wet, channel == 0), pressure, 0.0)
        pressure = pltpu.roll(pressure, 8, axis=1)
        for shift in (1, 2, 4):
            pressure = pressure + jnp.where(slot >= shift, pltpu.roll(pressure, 16 * shift, axis=1), 0.0)
        last = jnp.where(slot == GROUP - 1, pressure, 0.0)
        for shift in (16, 32, 64):
            last = last + pltpu.roll(last, shift, axis=1)
        pressure = pressure + carry
        carry = carry + last
        out_ref[g] = (weight + way * velocity) * near[g] - weight * own_ref[g] + way * pressure


def finish_kernel(
    last_step, levels, channels, height, state_ref, sum_ref, inverse_ref, depth_ref, own_ref, lon_one_ref, lon_two_ref, two_ref, one_ref, *refs
):
    if last_step:
        out_hbm, value_ref, north_ref, south_ref, edge_ref, sems = refs
    else:
        out_ref, columns_ref, outer_ref, inner_ref, value_ref, north_ref, south_ref, edge_ref = refs
        zero_pads(out_ref)
    whole, rest = divmod(levels, GROUP)
    level_rows = channels * height
    full = (height, 128)
    lane = lax.broadcasted_iota(jnp.int32, (SUB, 128), 1)
    row = lax.broadcasted_iota(jnp.int32, (SUB, 128), 0)
    at_edge = jnp.logical_or(lane == 0, lane == 127)
    at_south, at_north = row == 0, row == SUB - 1
    depth = depth_ref[...]
    halo_columns(levels, channels, own_ref, lon_one_ref, lon_two_ref, edge_ref)
    halo_rows(levels, channels, height, state_ref, one_ref, two_ref, True, north_ref)
    halo_rows(levels, channels, height, state_ref, one_ref, two_ref, False, south_ref)

    def forward(g, count, chosen, carried):
        edges = edge_ref[g]
        for slot in range(count):
            k = g * GROUP + slot
            inverse = inverse_ref[pl.ds(k * height, height), :]
            ratio = 4.0 * VERTICAL_MIX * inverse
            following = []
            for c, before in zip(chosen, carried):
                row = channels * k + c
                halves = []
                for half, (ref, at_row) in enumerate(((south_ref, at_south), (north_ref, at_north))):
                    at = pl.ds(k * level_rows + c * height + half * SUB, SUB)
                    place = GROUP * slot + 2 * c + half
                    columns = pltpu.roll(edges, 128 - (2 * place + 1), axis=1)
                    added = jnp.where(at_edge, columns, 0.0) + jnp.where(at_row, ref[pl.ds(row, 1), :], 0.0)
                    halves.append(sum_ref[at, :] + added)
                value = jnp.concatenate(halves, axis=0) * inverse - ratio * before
                value_ref[k, pl.ds(c * height, height), :] = value
                following.append(value)
            carried = tuple(following)
        return carried

    def out_copy(g, count, chosen, n):
        at = (pl.ds(g * GROUP, count), pl.ds(chosen[0] * height, len(chosen) * height))
        return pltpu.make_async_copy(value_ref.at[at], out_hbm.at[at], sems.at[n, g])

    def backward(g, count, chosen, solved, acc):
        for slot in reversed(range(count)):
            k = g * GROUP + slot
            upper = 4.0 * VERTICAL_MIX * inverse_ref[pl.ds(k * height, height), :]
            following = []
            for c, after in zip(chosen, solved):
                value = value_ref[k, pl.ds(c * height, height), :] - upper * after
                if last_step:
                    value_ref[k, pl.ds(c * height, height), :] = value
                else:
                    out_ref[pl.ds(PAD + k * level_rows + c * height, height), :] = value
                following.append(value)
            solved = tuple(following)
            if not last_step:
                acc = pack_columns(acc, solved, slot, lane)
        if not last_step:
            columns_ref[g] = acc
        return solved

    zero = jnp.zeros(full, jnp.float32)
    empty = jnp.zeros((SUB, 128), jnp.float32)
    passes = [(0, 1), (2, 3)] if last_step else [tuple(range(channels))]
    sizes = [GROUP] * whole + [rest]
    for n, chosen in enumerate(passes):
        carried = (zero,) * len(chosen)
        for g in range(whole + 1):
            carried = forward(g, sizes[g], chosen, carried)
        solved = (zero,) * len(chosen)
        for g in reversed(range(whole + 1)):
            acc = empty
            if not last_step and g == whole:
                acc = pack_columns(empty, [depth], rest, lane)
            solved = backward(g, sizes[g], chosen, solved, acc)
            if last_step:
                out_copy(g, sizes[g], chosen, n).start()
    if last_step:
        for n, chosen in enumerate(passes):
            for g in reversed(range(whole + 1)):
                out_copy(g, sizes[g], chosen, n).wait()
    else:
        write_rows(out_ref, depth, outer_ref, inner_ref, channels, height)


def in_vmem(count):
    return [pl.BlockSpec(memory_space=pltpu.VMEM)] * count


HBM = pl.BlockSpec(memory_space=pltpu.HBM)
PARAMS = pltpu.CompilerParams(vmem_limit_bytes=VMEM_LIMIT)


class Sizes:
    def __init__(self, shape):
        self.levels, self.channels, self.height, breadth = shape
        assert breadth == 128 and self.height == 2 * SUB and self.levels % GROUP
        self.own = (self.levels, self.channels, self.height)
        self.rows = self.levels * self.channels * self.height
        self.state = jax.ShapeDtypeStruct((self.rows + 2 * PAD, 128), jnp.float32)
        self.flat = jax.ShapeDtypeStruct((self.rows, 128), jnp.float32)
        self.solved = jax.ShapeDtypeStruct((self.levels, self.channels * self.height, 128), jnp.float32)
        self.depth = jax.ShapeDtypeStruct((self.height, 128), jnp.float32)
        self.inverse = jax.ShapeDtypeStruct((self.levels * self.height, 128), jnp.float32)
        self.columns = jax.ShapeDtypeStruct((self.levels // GROUP + 1, SUB, 128), jnp.float32)
        count = pl.cdiv(self.channels * self.levels + 1, SUB) * SUB
        self.edges = jax.ShapeDtypeStruct((count, 128), jnp.float32)
        self.messages = [self.columns, self.edges, self.edges]


def scratch(*shapes):
    return [pltpu.VMEM(s.shape, s.dtype) for s in shapes]


def pack(sizes, state, depth_levels):
    return pl.pallas_call(
        functools.partial(pack_kernel, *sizes.own),
        out_shape=[sizes.state, sizes.depth] + sizes.messages,
        in_specs=[HBM, HBM],
        out_specs=in_vmem(5),
        scratch_shapes=[pltpu.VMEM(sizes.depth.shape, jnp.int32), pltpu.SemaphoreType.DMA((CHUNKS + 1,))],
        compiler_params=PARAMS,
        name="pack",
    )(pltpu.with_memory_space_constraint(state, pltpu.HBM), pltpu.with_memory_space_constraint(depth_levels, pltpu.HBM))


def interior(sizes, table, state, depth):
    pressure = jax.ShapeDtypeStruct((GROUP * (sizes.height + 2 * PAD), 128), jnp.float32)
    return pl.pallas_call(
        functools.partial(interior_kernel, *sizes.own),
        out_shape=[sizes.flat, sizes.inverse],
        in_specs=[pl.BlockSpec(memory_space=pltpu.SMEM)] + in_vmem(2),
        out_specs=in_vmem(2),
        scratch_shapes=scratch(pressure),
        compiler_params=PARAMS,
        cost_estimate=pl.CostEstimate(flops=sizes.rows * 128 * 40, bytes_accessed=sizes.rows * 128 * 24, transcendentals=0),
        name="interior",
    )(table, state, depth)


def finish(sizes, last_step, state, summed, inverse, depth, own, lon_one, lon_two, one, two):
    if last_step:
        shapes, specs = sizes.solved, HBM
        extra = [pltpu.SemaphoreType.DMA((2, sizes.columns.shape[0]))]
    else:
        shapes, specs = [sizes.state] + sizes.messages, in_vmem(4)
        extra = []
    return pl.pallas_call(
        functools.partial(finish_kernel, last_step, *sizes.own),
        out_shape=shapes,
        in_specs=in_vmem(9),
        out_specs=specs,
        scratch_shapes=scratch(sizes.solved, sizes.edges, sizes.edges, sizes.columns) + extra,
        compiler_params=PARAMS,
        name="finish_last" if last_step else "finish",
    )(state, summed, inverse, depth, own, lon_one, lon_two, two, one)


def both_ways(pairs):
    return pairs + [(target, source) for source, target in pairs if target != source]


def exchange(columns, outer, inner):
    lons, lats = lax.axis_size("lon"), lax.axis_size("lat")

    def index(lon, lat):
        return lon * lats + lat

    outer_pairs, inner_pairs = [], []
    for lon in range(lons):
        outer_pairs += [(index(lon, lat), index(lon, lat + 1)) for lat in range(0, lats, 2)]
        inner_pairs += [(index(lon, lat), index(lon, lat + 1)) for lat in range(1, lats - 1, 2)]
        if lon < lons - 1 - lon:
            inner_pairs.append((index(lon, lats - 1), index(lons - 1 - lon, lats - 1)))
        if lon % 2 == 0:
            inner_pairs.append((index(lon, 0), index(lon + 1, 0)))
    two = lax.ppermute(inner, ("lon", "lat"), both_ways(inner_pairs))
    one = lax.ppermute(outer, ("lon", "lat"), both_ways(outer_pairs))
    lon_one = lax.ppermute(columns, "lon", both_ways([(i, i + 1) for i in range(0, lons, 2)]))
    lon_two = lax.ppermute(columns, "lon", both_ways([(i, (i + 1) % lons) for i in range(1, lons, 2)]))
    return lon_one, lon_two, one, two


def on_device(state, depth_levels):
    sizes = Sizes(state.shape)
    table = jnp.asarray(elimination_table(sizes.levels))
    current, depth, *messages = pack(sizes, state.reshape(sizes.flat.shape), depth_levels)
    for step_index in range(STEPS):
        last_step = step_index == STEPS - 1
        halos = exchange(*messages)
        summed, inverse = interior(sizes, table, current, depth)
        result = finish(sizes, last_step, current, summed, inverse, depth, messages[0], *halos)
        if not last_step:
            current, *messages = result
    return result.reshape(state.shape)


def solution(mesh):
    assert mesh.shape["lat"] % 2 == 0 and mesh.shape["lon"] % 2 == 0
    return jax.shard_map(
        on_device,
        mesh=mesh,
        in_specs=(P(None, None, "lat", "lon"), P("lat", "lon")),
        out_specs=P(None, None, "lat", "lon"),
        check_vma=False,
    )
```

```python
import functools

import jax
import jax.numpy as jnp
import numpy as np
from jax import lax
from jax.experimental import pallas as pl
from jax.experimental.pallas import tpu as pltpu
from jax.sharding import PartitionSpec as P

STEPS = 2
VERTICAL_MIX = 64.0
GROUP = 8
SUB = 8
PAD = 8
CHUNKS = 5
VMEM_LIMIT = 40 * 1024 * 1024


def elimination_table(levels):
    inside = np.zeros(levels)
    last = np.zeros(levels)
    upper = 0.0
    for k in range(levels):
        lower = VERTICAL_MIX if k else 0.0
        inside[k] = 1.0 / (1.0 + lower + VERTICAL_MIX - lower * upper)
        last[k] = 1.0 / (1.0 + lower - lower * upper)
        upper = VERTICAL_MIX * inside[k]
    return (np.stack([inside, last]) / 4).astype(np.float32)


def tile_pair(value, c, half):
    return value[c][half * SUB : (half + 1) * SUB, :]


def pack_columns(acc, values, slot, lane):
    for c in range(len(values)):
        for half in range(2):
            place = GROUP * slot + 2 * c + half
            turned = pltpu.roll(tile_pair(values, c, half), 2 * place + 1, axis=1)
            acc = jnp.where((lane >> 1) == place, turned, acc)
    return acc


def write_rows(state_ref, depth, outer_ref, inner_ref, channels, height):
    at_lat = lax.axis_index("lat")
    even = lax.rem(at_lat, 2) == 0
    fold = at_lat == lax.axis_size("lat") - 1
    shape = (SUB, 128)
    reverse = 127 - lax.broadcasted_iota(jnp.int32, shape, 1)
    line = lax.broadcasted_iota(jnp.int32, shape, 0)
    sign = jnp.where(lax.rem(line, channels) >= 2, -1.0, 1.0)
    rows = (state_ref.shape[0] - 2 * PAD) // height
    for start in range(0, rows, SUB):
        count = min(SUB, rows - start)
        at = pl.ds(start, SUB)
        base = PAD + start * height
        top = state_ref[pl.ds(base + height - 1, count, stride=height), :]
        bottom = state_ref[pl.ds(base, count, stride=height), :]
        if count < SUB:
            top = jnp.concatenate([top, jnp.broadcast_to(depth[-1:], (SUB - count, 128))], axis=0)
            bottom = jnp.concatenate([bottom, jnp.broadcast_to(depth[:1], (SUB - count, 128))], axis=0)
            sign = jnp.where(line >= count, 1.0, sign)
        mirrored = jnp.take_along_axis(top, reverse, axis=1) * sign
        outer_ref[at, :] = jnp.where(even, top, bottom)
        inner_ref[at, :] = jnp.where(even, bottom, jnp.where(fold, mirrored, top))


def zero_pads(ref):
    pad = jnp.zeros((PAD, 128), jnp.float32)
    ref[pl.ds(0, PAD), :] = pad
    ref[pl.ds(ref.shape[0] - PAD, PAD), :] = pad


def pack_kernel(levels, channels, height, state_hbm, levels_hbm, state_ref, depth_ref, own_ref, one_ref, two_ref, outer_ref, inner_ref, levels_ref, sems):
    level_rows = channels * height
    per_chunk = 2 * GROUP
    starts = range(0, levels, per_chunk)
    copies = []
    assert len(starts) <= CHUNKS
    for n, first in enumerate(starts):
        count = min(per_chunk, levels - first) * level_rows
        source = state_hbm.at[pl.ds(first * level_rows, count), :]
        target = state_ref.at[pl.ds(PAD + first * level_rows, count), :]
        copies.append(pltpu.make_async_copy(source, target, sems.at[n]))
    depth_copy = pltpu.make_async_copy(levels_hbm, levels_ref, sems.at[CHUNKS])
    depth_copy.start()
    for copy in copies:
        copy.start()
    zero_pads(state_ref)
    depth_copy.wait()
    depth = levels_ref[...].astype(jnp.float32)
    depth_ref[...] = depth
    for n, copy in enumerate(copies):
        copy.wait()
        write_columns(levels, channels, height, state_ref, depth, own_ref, one_ref, two_ref, [n])
    write_rows(state_ref, depth, outer_ref, inner_ref, channels, height)


def write_columns(levels, channels, height, state_ref, depth, own_ref, one_ref, two_ref, halves=None):
    lane = lax.broadcasted_iota(jnp.int32, (SUB, 128), 1)
    odd_lane = (lane & 1) == 1
    even = lax.rem(lax.axis_index("lon"), 2) == 0
    whole, rest = divmod(levels, GROUP)
    empty = jnp.zeros((SUB, 128), jnp.float32)

    def group(g):
        acc = empty
        if g == whole:
            acc = pack_columns(empty, [depth], rest, lane)
        for slot in range(GROUP if g < whole else rest):
            base = PAD + (g * GROUP + slot) * channels * height
            values = [state_ref[pl.ds(base + c * height, height), :] for c in range(channels)]
            acc = pack_columns(acc, values, slot, lane)
        own_ref[g] = acc
        return acc

    for half in halves or reversed(range(pl.cdiv(whole + 1, 2))):
        low = group(2 * half)
        high = group(2 * half + 1) if 2 * half < whole else empty
        first = jnp.where(odd_lane, low, pltpu.roll(high, 127, axis=1))
        last = jnp.where(odd_lane, pltpu.roll(high, 1, axis=1), low)
        one_ref[half] = jnp.where(even, last, first)
        two_ref[half] = jnp.where(even, first, last)


def interior_kernel(levels, channels, height, table_ref, state_ref, depth_ref, sum_ref, inverse_ref, pressure_ref):
    whole, rest = divmod(levels, GROUP)
    level_rows = channels * height
    full = (height, 128)
    column = lax.broadcasted_iota(jnp.int32, full, 1)
    row = lax.broadcasted_iota(jnp.int32, full, 0)
    at_west, at_east = column == 0, column == 127
    at_south, at_north = row == 0, row == height - 1
    at_lat = lax.axis_index("lat")
    total = height * lax.axis_size("lat")
    rotation = 0.4 + 1.6 * ((at_lat * height + row).astype(jnp.float32) + 0.5) / total
    depth = depth_ref[...]
    depth_east = jnp.where(at_east, 0.0, pltpu.roll(depth, 127, axis=1))
    depth_west = jnp.where(at_west, 0.0, pltpu.roll(depth, 1, axis=1))
    depth_north = jnp.where(at_north, 0.0, pltpu.roll(depth, height - 1, axis=0))
    depth_south = jnp.where(at_south, 0.0, pltpu.roll(depth, 1, axis=0))
    last_level = depth - 1.0
    slot_rows = height + 2 * PAD
    pad = jnp.zeros((PAD, 128), jnp.float32)
    for slot in range(GROUP):
        pressure_ref[pl.ds(slot * slot_rows, PAD), :] = pad
        pressure_ref[pl.ds(slot * slot_rows + PAD + height, PAD), :] = pad

    def group(g, count, pressure):
        for slot in range(count):
            k = g * GROUP + slot
            level = jnp.asarray(k, jnp.float32)
            inverse_ref[pl.ds(k * height, height), :] = jnp.where(
                last_level > level,
                table_ref[0, k],
                jnp.where(last_level == level, table_ref[1, k], 0.0),
            )
            base = PAD + (g * GROUP + slot) * level_rows

            def rows_at(c, shift):
                return state_ref[pl.ds(base + c * height + shift, height), :]

            values = [rows_at(c, 0) for c in range(channels)]
            pressure = pressure + jnp.where(depth > level, 0.3 * values[1] - 0.1 * values[0], 0.0)
            at = slot * slot_rows + PAD
            pressure_ref[pl.ds(at, height), :] = pressure
            slope_east = jnp.where(at_east, 0.0, pltpu.roll(pressure, 127, axis=1)) - jnp.where(
                at_west, 0.0, pltpu.roll(pressure, 1, axis=1)
            )
            slope_north = pressure_ref[pl.ds(at + 1, height), :] - pressure_ref[pl.ds(at - 1, height), :]
            east = [pltpu.roll(v, 127, axis=1) for v in values]
            west = [pltpu.roll(v, 1, axis=1) for v in values]
            north = [rows_at(c, 1) for c in range(channels)]
            south = [rows_at(c, -1) for c in range(channels)]
            weights = [
                jnp.where(d > level, 0.6, 0.0) for d in (depth_east, depth_west, depth_north, depth_south)
            ]
            from_east = jnp.where(at_east, 0.0, weights[0] - east[2])
            from_west = jnp.where(at_west, 0.0, weights[1] + west[2])
            from_north = jnp.where(at_north, 0.0, weights[2] - north[3])
            from_south = jnp.where(at_south, 0.0, weights[3] + south[3])
            centre = 4.0 - ((weights[0] + weights[1]) + (weights[2] + weights[3]))
            forces = [None, None, rotation * values[3] - slope_east, -rotation * values[2] - slope_north]
            for c in range(channels):
                moved = (centre * values[c] + from_east * east[c]) + (
                    from_west * west[c] + from_north * north[c]
                )
                moved = moved + from_south * south[c]
                if forces[c] is not None:
                    moved = moved + forces[c]
                sum_ref[pl.ds((g * GROUP + slot) * level_rows + c * height, height), :] = moved
        return pressure

    pressure = jnp.zeros(full, jnp.float32)
    for g in range(whole + 1):
        pressure = group(g, GROUP if g < whole else rest, pressure)


def halo_rows(levels, channels, height, state_ref, one_ref, two_ref, northern, out_ref):
    edge = height - 1 if northern else 0
    way = -1.0 if northern else 1.0

    at_lat = lax.axis_index("lat")
    even = lax.rem(at_lat, 2) == 0

    def halo(at, count, stride):
        one = one_ref[pl.ds(at, count, stride=stride), :]
        two = two_ref[pl.ds(at, count, stride=stride), :]
        if northern:
            return jnp.where(even, one, two)
        return jnp.where(even, jnp.where(at_lat == 0, 0.0, two), one)

    depth = halo(channels * levels, 1, 1)
    carry = jnp.zeros((1, 128), jnp.float32)
    for start in range(0, levels, SUB):
        count = min(SUB, levels - start)
        near = [halo(channels * start + c, count, channels) for c in range(channels)]
        level = lax.broadcasted_iota(jnp.int32, (count, 128), 0)
        wet = (level + start).astype(jnp.float32) < depth
        weight = jnp.where(wet, 0.6, 0.0)
        pressure = jnp.where(wet, 0.3 * near[1] - 0.1 * near[0], 0.0)
        if count < SUB:
            pressure = jnp.concatenate([pressure, jnp.zeros((SUB - count, 128), jnp.float32)], axis=0)
        level = lax.broadcasted_iota(jnp.int32, (SUB, 128), 0)
        for shift in (1, 2, 4):
            pressure = pressure + jnp.where(level >= shift, pltpu.roll(pressure, shift, axis=0), 0.0)
        pressure = pressure + carry
        carry = pressure[SUB - 1 : SUB, :]
        factor = weight + way * near[3]
        for c in range(channels):
            at = PAD + (start * channels + c) * height + edge
            own = state_ref[pl.ds(at, count, stride=channels * height), :]
            added = factor * near[c] - weight * own
            if c == 3:
                added = added + way * pressure[:count]
            out_ref[pl.ds(start * channels + c, count, stride=channels), :] = added


def halo_columns(levels, channels, own_ref, one_ref, two_ref, out_ref):
    assert channels == 4 and GROUP == 8
    shape = (SUB, 128)
    lane = lax.broadcasted_iota(jnp.int32, shape, 1)
    western = (lane & 1) == 1
    way = jnp.where(western, 1.0, -1.0)
    channel = (lane >> 2) & 3
    slot = lane >> 4

    even = lax.rem(lax.axis_index("lon"), 2) == 0

    def halo(g):
        one, two = one_ref[g // 2], two_ref[g // 2]
        east = jnp.where(even, one, two)
        west = jnp.where(even, two, one)
        if g % 2 == 0:
            east, west = pltpu.roll(east, 127, axis=1), pltpu.roll(west, 1, axis=1)
        return jnp.where(western, west, east)

    whole, rest = divmod(levels, GROUP)
    groups = whole + 1
    near = [halo(g) for g in range(groups)]
    depth = jnp.where(lane >> 2 == channels * rest, near[whole], 0.0)
    for shift in (4, 8, 16, 32, 64):
        depth = depth + pltpu.roll(depth, shift, axis=1)
    carry = jnp.zeros(shape, jnp.float32)
    for g in range(groups):
        wet = (slot + g * GROUP).astype(jnp.float32) < depth
        weight = jnp.where(wet, 0.6, 0.0)
        velocity = jnp.where(channel == 2, near[g], 0.0)
        velocity = velocity + pltpu.roll(velocity, 4, axis=1)
        velocity = velocity + pltpu.roll(velocity, 120, axis=1)
        pressure = 0.3 * pltpu.roll(near[g], 124, axis=1) - 0.1 * near[g]
        pressure = jnp.where(jnp.logical_and(wet, channel == 0), pressure, 0.0)
        pressure = pltpu.roll(pressure, 8, axis=1)
        for shift in (1, 2, 4):
            pressure = pressure + jnp.where(slot >= shift, pltpu.roll(pressure, 16 * shift, axis=1), 0.0)
        last = jnp.where(slot == GROUP - 1, pressure, 0.0)
        for shift in (16, 32, 64):
            last = last + pltpu.roll(last, shift, axis=1)
        pressure = pressure + carry
        carry = carry + last
        out_ref[g] = (weight + way * velocity) * near[g] - weight * own_ref[g] + way * pressure


def finish_kernel(
    last_step, levels, channels, height, state_ref, sum_ref, inverse_ref, depth_ref, own_ref, lon_one_ref, lon_two_ref, one_ref, two_ref, *refs
):
    if last_step:
        out_hbm, value_ref, north_ref, south_ref, edge_ref, sems = refs
    else:
        out_ref, columns_ref, facing_one_ref, facing_two_ref, outer_ref, inner_ref, value_ref, north_ref, south_ref, edge_ref = refs
        zero_pads(out_ref)
    whole, rest = divmod(levels, GROUP)
    level_rows = channels * height
    full = (height, 128)
    lane = lax.broadcasted_iota(jnp.int32, (SUB, 128), 1)
    row = lax.broadcasted_iota(jnp.int32, (SUB, 128), 0)
    at_edge = jnp.logical_or(lane == 0, lane == 127)
    at_south, at_north = row == 0, row == SUB - 1
    depth = depth_ref[...]
    halo_columns(levels, channels, own_ref, lon_one_ref, lon_two_ref, edge_ref)
    halo_rows(levels, channels, height, state_ref, one_ref, two_ref, True, north_ref)
    halo_rows(levels, channels, height, state_ref, one_ref, two_ref, False, south_ref)

    def forward(g, count, chosen, carried):
        edges = edge_ref[g]
        for slot in range(count):
            k = g * GROUP + slot
            inverse = inverse_ref[pl.ds(k * height, height), :]
            ratio = 4.0 * VERTICAL_MIX * inverse
            following = []
            for c, before in zip(chosen, carried):
                row = channels * k + c
                halves = []
                for half, (ref, at_row) in enumerate(((south_ref, at_south), (north_ref, at_north))):
                    at = pl.ds(k * level_rows + c * height + half * SUB, SUB)
                    place = GROUP * slot + 2 * c + half
                    columns = pltpu.roll(edges, 128 - (2 * place + 1), axis=1)
                    added = jnp.where(at_edge, columns, 0.0) + jnp.where(at_row, ref[pl.ds(row, 1), :], 0.0)
                    halves.append(sum_ref[at, :] + added)
                value = jnp.concatenate(halves, axis=0) * inverse - ratio * before
                value_ref[k, pl.ds(c * height, height), :] = value
                following.append(value)
            carried = tuple(following)
        return carried

    def out_copy(g, count, chosen, n):
        at = (pl.ds(g * GROUP, count), pl.ds(chosen[0] * height, len(chosen) * height))
        return pltpu.make_async_copy(value_ref.at[at], out_hbm.at[at], sems.at[n, g])

    def backward(g, count, chosen, solved):
        for slot in reversed(range(count)):
            k = g * GROUP + slot
            upper = 4.0 * VERTICAL_MIX * inverse_ref[pl.ds(k * height, height), :]
            following = []
            for c, after in zip(chosen, solved):
                value = value_ref[k, pl.ds(c * height, height), :] - upper * after
                if last_step:
                    value_ref[k, pl.ds(c * height, height), :] = value
                else:
                    out_ref[pl.ds(PAD + k * level_rows + c * height, height), :] = value
                following.append(value)
            solved = tuple(following)
        return solved

    zero = jnp.zeros(full, jnp.float32)
    passes = [(0, 1), (2, 3)] if last_step else [tuple(range(channels))]
    sizes = [GROUP] * whole + [rest]
    for n, chosen in enumerate(passes):
        carried = (zero,) * len(chosen)
        for g in range(whole + 1):
            carried = forward(g, sizes[g], chosen, carried)
        solved = (zero,) * len(chosen)
        for g in reversed(range(whole + 1)):
            solved = backward(g, sizes[g], chosen, solved)
            if last_step:
                out_copy(g, sizes[g], chosen, n).start()
    if last_step:
        for n, chosen in enumerate(passes):
            for g in reversed(range(whole + 1)):
                out_copy(g, sizes[g], chosen, n).wait()
    else:
        write_columns(levels, channels, height, out_ref, depth, columns_ref, facing_one_ref, facing_two_ref)
        write_rows(out_ref, depth, outer_ref, inner_ref, channels, height)


def in_vmem(count):
    return [pl.BlockSpec(memory_space=pltpu.VMEM)] * count


HBM = pl.BlockSpec(memory_space=pltpu.HBM)
PARAMS = pltpu.CompilerParams(vmem_limit_bytes=VMEM_LIMIT)


class Sizes:
    def __init__(self, shape):
        self.levels, self.channels, self.height, breadth = shape
        assert breadth == 128 and self.height == 2 * SUB and self.levels % GROUP
        self.own = (self.levels, self.channels, self.height)
        self.rows = self.levels * self.channels * self.height
        self.state = jax.ShapeDtypeStruct((self.rows + 2 * PAD, 128), jnp.float32)
        self.flat = jax.ShapeDtypeStruct((self.rows, 128), jnp.float32)
        self.solved = jax.ShapeDtypeStruct((self.levels, self.channels * self.height, 128), jnp.float32)
        self.depth = jax.ShapeDtypeStruct((self.height, 128), jnp.float32)
        self.inverse = jax.ShapeDtypeStruct((self.levels * self.height, 128), jnp.float32)
        self.columns = jax.ShapeDtypeStruct((self.levels // GROUP + 1, SUB, 128), jnp.float32)
        count = pl.cdiv(self.channels * self.levels + 1, SUB) * SUB
        self.edges = jax.ShapeDtypeStruct((count, 128), jnp.float32)
        facing = jax.ShapeDtypeStruct((pl.cdiv(self.columns.shape[0], 2), SUB, 128), jnp.float32)
        self.messages = [self.columns, facing, facing, self.edges, self.edges]


def scratch(*shapes):
    return [pltpu.VMEM(s.shape, s.dtype) for s in shapes]


def pack(sizes, state, depth_levels):
    return pl.pallas_call(
        functools.partial(pack_kernel, *sizes.own),
        out_shape=[sizes.state, sizes.depth] + sizes.messages,
        in_specs=[HBM, HBM],
        out_specs=in_vmem(7),
        scratch_shapes=[pltpu.VMEM(sizes.depth.shape, jnp.int32), pltpu.SemaphoreType.DMA((CHUNKS + 1,))],
        compiler_params=PARAMS,
        name="pack",
    )(pltpu.with_memory_space_constraint(state, pltpu.HBM), pltpu.with_memory_space_constraint(depth_levels, pltpu.HBM))


def interior(sizes, table, state, depth):
    pressure = jax.ShapeDtypeStruct((GROUP * (sizes.height + 2 * PAD), 128), jnp.float32)
    return pl.pallas_call(
        functools.partial(interior_kernel, *sizes.own),
        out_shape=[sizes.flat, sizes.inverse],
        in_specs=[pl.BlockSpec(memory_space=pltpu.SMEM)] + in_vmem(2),
        out_specs=in_vmem(2),
        scratch_shapes=scratch(pressure),
        compiler_params=PARAMS,
        cost_estimate=pl.CostEstimate(flops=sizes.rows * 128 * 40, bytes_accessed=sizes.rows * 128 * 24, transcendentals=0),
        name="interior",
    )(table, state, depth)


def finish(sizes, last_step, state, summed, inverse, depth, own, lon_one, lon_two, one, two):
    if last_step:
        shapes, specs = sizes.solved, HBM
        extra = [pltpu.SemaphoreType.DMA((2, sizes.columns.shape[0]))]
    else:
        shapes, specs = [sizes.state] + sizes.messages, in_vmem(6)
        extra = []
    return pl.pallas_call(
        functools.partial(finish_kernel, last_step, *sizes.own),
        out_shape=shapes,
        in_specs=in_vmem(9),
        out_specs=specs,
        scratch_shapes=scratch(sizes.solved, sizes.edges, sizes.edges, sizes.columns) + extra,
        compiler_params=PARAMS,
        name="finish_last" if last_step else "finish",
    )(state, summed, inverse, depth, own, lon_one, lon_two, one, two)


def both_ways(pairs):
    return pairs + [(target, source) for source, target in pairs if target != source]


def exchange(lon_first, lon_second, outer, inner):
    lons, lats = lax.axis_size("lon"), lax.axis_size("lat")

    def index(lon, lat):
        return lon * lats + lat

    outer_pairs, inner_pairs = [], []
    for lon in range(lons):
        outer_pairs += [(index(lon, lat), index(lon, lat + 1)) for lat in range(0, lats, 2)]
        inner_pairs += [(index(lon, lat), index(lon, lat + 1)) for lat in range(1, lats - 1, 2)]
        if lon < lons - 1 - lon:
            inner_pairs.append((index(lon, lats - 1), index(lons - 1 - lon, lats - 1)))
        if lon % 2 == 0:
            inner_pairs.append((index(lon, 0), index(lon + 1, 0)))
    two = lax.ppermute(inner, ("lon", "lat"), both_ways(inner_pairs))
    one = lax.ppermute(outer, ("lon", "lat"), both_ways(outer_pairs))
    lon_one = lax.ppermute(lon_first, "lon", both_ways([(i, i + 1) for i in range(0, lons, 2)]))
    lon_two = lax.ppermute(lon_second, "lon", both_ways([(i, (i + 1) % lons) for i in range(1, lons, 2)]))
    return lon_one, lon_two, one, two


def on_device(state, depth_levels):
    sizes = Sizes(state.shape)
    table = jnp.asarray(elimination_table(sizes.levels))
    current, depth, *messages = pack(sizes, state.reshape(sizes.flat.shape), depth_levels)
    for step_index in range(STEPS):
        last_step = step_index == STEPS - 1
        own, *messages = messages
        halos = exchange(*messages)
        summed, inverse = interior(sizes, table, current, depth)
        result = finish(sizes, last_step, current, summed, inverse, depth, own, *halos)
        if not last_step:
            current, *messages = result
    return result.reshape(state.shape)


def solution(mesh):
    assert mesh.shape["lat"] % 2 == 0 and mesh.shape["lon"] % 2 == 0
    return jax.shard_map(
        on_device,
        mesh=mesh,
        in_specs=(P(None, None, "lat", "lon"), P("lat", "lon")),
        out_specs=P(None, None, "lat", "lon"),
        check_vma=False,
    )
```
